256 devices in a mesh: dp: 32 (over x, z), vocab: 8 (over y, core).
Axes of the slice: x: 4, y: 4, z: 8, core: 2. Of those that a mesh axis runs over, the one named last changes fastest.
Arguments:
- hidden_states: bfloat16 [8192, 8192], P('dp', 'vocab'), may hold values from -100 to 100, as said below
- logits: bfloat16 [8192, 128256], P('dp', 'vocab'), may hold values from -20 to 260
- targets: int32 [8192], P('dp'), may hold values from 0 to 128255
- input_proj: bfloat16 [8192, 64], P('vocab'), may hold values from -0.0625 to 0.0625
- output_proj: bfloat16 [128256, 64], P('vocab'), may hold values from -6 to 6
- query_ids: int32 [64], replicated, may hold values from 0 to 63
Outputs:
- scores: float32 [64, 64], P('dp')
The draws below stay inside these ranges and needn't reach their ends.
Inputs may be any that keep to these rules, and one draw needn't show every extreme that they name: `hidden_states`: hidden states of order one to ten.
All inputs are finite; a program needn't handle non-finite values.
Results may differ from the reference program's by a relative error of at most 0.0003.
Values may be sent and summed in bfloat16 or wider, within the bound.
A program may use at most 64 MiB of HBM per device.

```python
import math
import jax
import jax.numpy as jnp
import numpy as np
from jax import lax

D = 8192
VOCAB = 128256
R_IN = 64
R_OUT = 64
QUERIES = 64
SEQ = 128
EXAMPLES = 64
TOKENS = 8192


def draw_hidden_states(key, part):
    key = jax.random.fold_in(key, 11)
    key_rows, key_cols, key_main = jax.random.split(key, 3)
    half_range = math.log(10.0) / 2.0
    main = jnp.clip(jax.random.normal(key_main, (TOKENS, D), jnp.float32), -5.0, 5.0)
    row_scale = jnp.exp(jax.random.uniform(key_rows, (TOKENS, 1), jnp.float32, 0.0, half_range))
    col_scale = jnp.exp(jax.random.uniform(key_cols, (1, D), jnp.float32, 0.0, half_range))
    return (main * row_scale * col_scale).astype(jnp.bfloat16)


def draw_logits(key, part):
    key = jax.random.fold_in(key, 23)
    key_main = jax.random.fold_in(key, 0)
    columns = lax.broadcasted_iota(jnp.int32, (1, VOCAB), 1)
    ramp = math.log(3.0) * columns.astype(jnp.float32) / VOCAB
    values = 3.0 * jnp.clip(jax.random.normal(key_main, (TOKENS, VOCAB), jnp.float32), -6.0, 6.0) + ramp
    return values.astype(jnp.bfloat16)


def touch_ends(values, own_key, low, largest):
    spot = [jax.random.randint(jax.random.fold_in(own_key, axis), (), 0, length) for axis, length in enumerate(values.shape)]
    main_axis = values.shape.index(max(values.shape))
    next_to = spot[:main_axis] + [(spot[main_axis] + 1) % values.shape[main_axis]] + spot[main_axis + 1:]
    return values.at[tuple(spot)].set(low).at[tuple(next_to)].set(largest)


def block_scale(stream_key, extent, cuts, low, largest):
    def one(dim, parts):
        steps = jax.random.uniform(jax.random.fold_in(jax.random.fold_in(stream_key, 6), dim), (parts,), jnp.float32, low / len(cuts), largest / len(cuts))
        return jnp.repeat(jnp.exp(steps), extent[dim] // parts).reshape((-1,) + (1,) * (len(extent) - dim - 1))

    level = one(*cuts[0])
    for cut in cuts[1:]:
        level = level * one(*cut)
    return level


def wide_ids(own_key, shape, number_of, skew):
    loads = [min(1 << octave, number_of + 1 - (1 << octave)) * (1 << 20) // math.isqrt((1 << octave) ** skew) + 1 for octave in range((number_of + 1).bit_length()) if 1 << octave <= number_of]
    width = 1 + sum(loads) // (1 << 30)
    table = np.cumsum(np.array([max(1, weight // width) for weight in loads]))
    lot = jax.random.randint(jax.random.fold_in(own_key, 1), shape, 0, int(table[len(loads) - 1]))
    start = jnp.left_shift(1, jnp.searchsorted(jnp.asarray(table, jnp.int32), lot, side="right").astype(jnp.int32))
    rank = start - 1 + jax.random.randint(jax.random.fold_in(own_key, 4), shape, 0, 1 << 30) % jnp.minimum(start, number_of + 1 - start)
    return jax.random.permutation(jax.random.fold_in(own_key, 2), number_of)[rank].astype(jnp.int32)


def centred(rng, extent, width, limit, cuts=(), held_as=jnp.bfloat16):
    drawn = jax.random.normal(rng, extent, jnp.float32) * width
    if len(cuts) > 0:
        drawn = block_scale(rng, extent, cuts, -0.22, 0.18) * drawn
    return jnp.clip(drawn, min=-limit, max=limit).astype(held_as)


def setup_inputs(seed: int = 0) -> dict:
    arg_keys = jax.random.split(jax.random.key(seed), 7)
    hidden_states = draw_hidden_states(jax.random.fold_in(arg_keys[6], 71), 0)
    logits = draw_logits(jax.random.fold_in(arg_keys[6], 71), 0)
    targets = touch_ends(wide_ids(arg_keys[2], (TOKENS,), VOCAB, 2), jax.random.fold_in(arg_keys[2], 3), 0, VOCAB - 1).astype(jnp.int32)
    input_proj = centred(arg_keys[3], (D, R_IN), D ** -0.5, 0.0625, ((0, 8),))
    output_proj = centred(arg_keys[4], (VOCAB, R_OUT), 1.0, 6.0, ((0, 8),))
    query_ids = touch_ends(jax.random.randint(arg_keys[5], (QUERIES,), 0, EXAMPLES), jax.random.fold_in(arg_keys[5], 1), 0, EXAMPLES - 1).astype(jnp.int32)
    return {"hidden_states": hidden_states, "logits": logits, "targets": targets, "input_proj": input_proj, "output_proj": output_proj, "query_ids": query_ids}


def one_example(pieces, input_proj, output_proj):
    block, states, wanted = pieces
    values = block.astype(jnp.float32)
    row_max = lax.optimization_barrier(jnp.max(values, axis=1, keepdims=True))
    exp_terms = jnp.exp(values - row_max)
    row_total = lax.optimization_barrier(jnp.sum(exp_terms, axis=1, keepdims=True))
    columns = lax.broadcasted_iota(jnp.int32, values.shape, 1)
    hit = (columns == wanted[:, None].astype(jnp.int32)).astype(jnp.float32)
    out_grad = (exp_terms / row_total - hit).astype(jnp.bfloat16)
    out_low = jnp.dot(out_grad.astype(jnp.float32), output_proj.astype(jnp.float32), precision=lax.Precision.HIGHEST)
    in_low = jnp.dot(states.astype(jnp.float32), input_proj.astype(jnp.float32), precision=lax.Precision.HIGHEST)
    return jnp.dot(in_low.T, out_low, precision=lax.Precision.HIGHEST)

def reference(hidden_states, logits, targets, input_proj, output_proj, query_ids):
    blocks = logits.reshape(EXAMPLES, SEQ, VOCAB)
    states = hidden_states.reshape(EXAMPLES, SEQ, D)
    wanted = targets.reshape(EXAMPLES, SEQ)
    example_grad = lax.map(lambda p: one_example(p, input_proj, output_proj), (blocks, states, wanted))
    flat = example_grad.reshape(EXAMPLES, R_IN * R_OUT)
    chosen = jnp.take(flat, query_ids.astype(jnp.int32), axis=0)
    dots = jnp.dot(flat, chosen.T, precision=lax.Precision.HIGHEST)
    self_sq = lax.optimization_barrier(jnp.sum(flat * flat, axis=1))
    query_sq = lax.optimization_barrier(jnp.sum(chosen * chosen, axis=1))
    return dots * lax.rsqrt(self_sq + 1e-06)[:, None] * lax.rsqrt(query_sq + 1e-06)[None, :]
```

```python
import functools

import jax
import jax.numpy as jnp
from jax import lax
from jax.experimental import pallas as pl
from jax.experimental.pallas import tpu as pltpu
from jax.sharding import PartitionSpec as P

MESH = pl.DeviceIdType.MESH
F32 = jnp.float32
BF16 = jnp.bfloat16
SEQ = 128
LOG2E = 1.4426950408889634
HIGH = lax.Precision.HIGHEST
CHUNK = 2048
STEP = 256


def dot_t(a, b, precision=None):
    return lax.dot_general(
        a, b, (((1,), (1,)), ((), ())), precision=precision, preferred_element_type=F32
    )


def kernel(
    n_dp,
    n_voc,
    logits_hbm,
    proj_hbm,
    hidden_hbm,
    inproj_hbm,
    targets_ref,
    query_ref,
    out_ref,
    lbuf,
    ebuf,
    pbuf,
    hbuf,
    ibuf,
    in_part,
    in_parts,
    in_block,
    in_full,
    stat_src,
    stats,
    eg_src,
    eg_parts,
    slice_src,
    slices,
    sum_src,
    sums,
    load_sems,
    logit_sems,
    send_sems,
    recv_sems,
):
    rows, tokens = lbuf.shape
    me_d = lax.axis_index("dp")
    me_v = lax.axis_index("vocab")
    starts = list(range(0, rows, CHUNK))
    sizes = [min(CHUNK, rows - s) for s in starts]
    n_chunks = len(starts)

    loads = [
        pltpu.make_async_copy(hidden_hbm, hbuf, load_sems.at[0]),
        pltpu.make_async_copy(inproj_hbm, ibuf, load_sems.at[1]),
        pltpu.make_async_copy(proj_hbm, pbuf, load_sems.at[2]),
    ]
    chunk_loads = [
        pltpu.make_async_copy(
            logits_hbm.at[pl.ds(s, w)], lbuf.at[pl.ds(s, w)], logit_sems.at[c]
        )
        for c, (s, w) in enumerate(zip(starts, sizes))
    ]
    loads[0].start()
    loads[1].start()
    for copy in chunk_loads:
        copy.start()
    loads[2].start()

    def other_v(j):
        return lax.rem(me_v + j, n_voc)

    def other_d(j):
        return lax.rem(me_d + j, n_dp)

    barrier = pltpu.get_barrier_semaphore()

    def greet_v(j, carry):
        pl.semaphore_signal(
            barrier, inc=1, device_id=(me_d, other_v(j)), device_id_type=MESH
        )
        return carry

    def greet_d(j, carry):
        pl.semaphore_signal(
            barrier, inc=1, device_id=(other_d(j), me_v), device_id_type=MESH
        )
        return carry

    lax.fori_loop(1, n_voc, greet_v, 0)
    lax.fori_loop(1, n_dp, greet_d, 0)

    def send_v(src_of, dst, rnd):
        def one(j, carry):
            to = other_v(j)
            pltpu.make_async_remote_copy(
                src_ref=src_of(to),
                dst_ref=dst.at[me_v],
                send_sem=send_sems.at[rnd],
                recv_sem=recv_sems.at[rnd],
                device_id=(me_d, to),
                device_id_type=MESH,
            ).start()
            return carry

        lax.fori_loop(1, n_voc, one, 0)

    def wait_blocks(dst, sem, n):
        ref = dst.at[pl.ds(0, n - 1)]
        pltpu.make_async_copy(ref, ref, sem).wait()

    loads[0].wait()
    loads[1].wait()
    part = dot_t(ibuf[...], hbuf[...])
    in_part[...] = part.reshape(in_part.shape)
    in_parts[me_v] = in_part[me_v]

    pl.semaphore_wait(barrier, n_voc + n_dp - 2)
    send_v(lambda to: in_part.at[to], in_parts, 0)

    tgt = targets_ref[...] - me_v * rows
    col16 = lax.broadcasted_iota(jnp.int32, (16, tokens), 0)

    run_max = jnp.full((1, tokens), -1e30, F32)
    run_sum = jnp.zeros((8, tokens), F32)
    picked = jnp.zeros((16, tokens), BF16)
    chunk_max = []
    for c, (s, w) in enumerate(zip(starts, sizes)):
        chunk_loads[c].wait()
        group = jnp.clip((tgt - s) >> 4, -1, CHUNK // 16)
        group = jnp.broadcast_to(group, (16, tokens)).astype(F32).astype(BF16)

        n_full = w // 128
        tail = w % 128

        def scan(i, carry, s=s, count=8):
            top, sel, g = carry
            x = lbuf[pl.ds(pl.multiple_of(s + i * 128, 16), count * 16), :]
            for j in range(count):
                xj = x[16 * j : 16 * j + 16]
                top = jnp.maximum(top, xj)
                sel = jnp.where(g == BF16(j), xj, sel)
            return top, sel, g - BF16(8)

        top = jnp.full((16, tokens), -1e30, BF16)
        carry = lax.fori_loop(0, n_full, scan, (top, picked, group))
        if tail:
            carry = scan(n_full, carry, count=tail // 16)
        top, picked, _ = carry
        here = jnp.max(top.astype(F32), axis=0, keepdims=True)
        new_max = jnp.maximum(run_max, here)
        run_sum = run_sum * jnp.exp2((run_max - new_max) * LOG2E)
        run_max = new_max
        chunk_max.append(new_max)

        def exps(i, acc, s=s, count=128, new_max=new_max):
            at = pl.ds(pl.multiple_of(s + i * 128, 16), count)
            e = jnp.exp2((lbuf[at, :].astype(F32) - new_max) * LOG2E)
            ebuf[at, :] = e
            return acc + jnp.sum(e.reshape(count // 8, 8, tokens), axis=0)

        run_sum = lax.fori_loop(0, n_full, exps, run_sum)
        if tail:
            run_sum = exps(n_full, run_sum, count=tail)

        if c == 2:
            wait_blocks(in_parts, recv_sems.at[0], n_voc)
            block = jnp.sum(in_parts[...], axis=0)
            in_block[...] = block
            in_full[me_v] = block
            send_v(lambda to: in_block, in_full, 1)

    total_here = jnp.sum(run_sum, axis=0, keepdims=True)
    stat_src[0:1, :] = run_max[:, :128]
    stat_src[1:2, :] = run_max[:, 128:]
    stat_src[2:3, :] = total_here[:, :128]
    stat_src[3:4, :] = total_here[:, 128:]
    stats[me_v] = stat_src[...]
    send_v(lambda to: stat_src, stats, 2)

    loads[2].wait()
    block_of = tgt >> 8
    lane_of = tgt & 255
    pick = (lax.broadcasted_iota(jnp.int32, (256, tokens), 0) == lane_of).astype(F32).astype(BF16)

    def gather(k, acc):
        cols = pbuf[:, pl.ds(pl.multiple_of(k * 256, 256), 256)]
        found = jnp.dot(cols, pick, preferred_element_type=F32)
        return jnp.where(block_of == k, found, acc)

    n_blocks = rows // 256
    rest = rows % 256
    wanted = lax.fori_loop(0, n_blocks, gather, jnp.zeros((pbuf.shape[0], tokens), F32))
    if rest:
        found = jnp.dot(pbuf[:, n_blocks * 256 :], pick[:rest], preferred_element_type=F32)
        wanted = jnp.where(block_of == n_blocks, found, wanted)
    at_target = jnp.sum(
        jnp.where(col16 == (tgt & 15), picked.astype(F32), 0.0), axis=0, keepdims=True
    )

    wait_blocks(stats, recv_sems.at[2], n_voc)
    all_stats = stats[...]
    every_max = jnp.concatenate([all_stats[:, 0, :], all_stats[:, 1, :]], axis=1)
    every_sum = jnp.concatenate([all_stats[:, 2, :], all_stats[:, 3, :]], axis=1)
    row_max = jnp.max(every_max, axis=0, keepdims=True)
    row_total = jnp.sum(
        every_sum * jnp.exp2((every_max - row_max) * LOG2E), axis=0, keepdims=True
    )
    inverse = 1.0 / row_total
    scale = [jnp.exp2((m - row_max) * LOG2E) * inverse for m in chunk_max]

    chunk_of = tgt >> 11
    target_max = chunk_max[0]
    target_scale = scale[0]
    for c in range(1, n_chunks):
        target_max = jnp.where(chunk_of == c, chunk_max[c], target_max)
        target_scale = jnp.where(chunk_of == c, scale[c], target_scale)
    p_target = jnp.exp2((at_target - target_max) * LOG2E) * target_scale
    fix = (p_target - 1.0).astype(BF16).astype(F32) - p_target.astype(BF16).astype(F32)
    fix = jnp.where((tgt >= 0) & (tgt < rows), fix, 0.0)

    out_low = wanted * fix
    for c, (s, w) in enumerate(zip(starts, sizes)):

        def project(i, acc, s=s, c=c, count=STEP):
            first = pl.multiple_of(s + i * STEP, STEP)
            probs = (ebuf[pl.ds(first, count), :] * scale[c]).astype(BF16)
            cols = pbuf[:, pl.ds(first, count)]
            return acc + jnp.dot(cols, probs, preferred_element_type=F32)

        out_low = lax.fori_loop(0, w // STEP, project, out_low)
        if w % STEP:
            out_low = project(w // STEP, out_low, count=w % STEP)

    wait_blocks(in_full, recv_sems.at[1], n_voc)
    in_low = in_full[...].reshape(in_full.shape[0] * in_full.shape[1], tokens)
    grads = [
        dot_t(in_low[:, t : t + SEQ], out_low[:, t : t + SEQ], HIGH)
        for t in range(0, tokens, SEQ)
    ]
    eg_src[...] = jnp.concatenate(grads, axis=1).reshape(eg_src.shape)
    eg_parts[me_v] = eg_src[me_v]
    send_v(lambda to: eg_src.at[to], eg_parts, 3)

    query = query_ref[...]
    query_d = query >> 1
    query_odd = (query & 1) == 1
    lane = lax.broadcasted_iota(jnp.int32, (128, 64), 0)
    place = jnp.concatenate(
        [(lane == query_d).astype(F32), (lane == query_d + 32).astype(F32)], axis=1
    )
    half = lax.broadcasted_iota(jnp.int32, (8, 128), 1) // 64
    halves = (half == lax.broadcasted_iota(jnp.int32, (8, 128), 0)).astype(F32)

    wait_blocks(eg_parts, recv_sems.at[3], n_voc)
    mine = jnp.sum(eg_parts[...], axis=0)
    slice_src[...] = mine
    slices[pl.ds(pl.multiple_of(me_d * 8, 8), 8), :] = mine

    def share(j, carry):
        pltpu.make_async_remote_copy(
            src_ref=slice_src,
            dst_ref=slices.at[pl.ds(pl.multiple_of(me_d * 8, 8), 8)],
            send_sem=send_sems.at[4],
            recv_sem=recv_sems.at[4],
            device_id=(other_d(j), me_v),
            device_id_type=MESH,
        ).start()
        return carry

    lax.fori_loop(1, n_dp, share, 0)
    swapped = jnp.concatenate([mine[:, 64:], mine[:, :64]], axis=1)
    ref = slices.at[pl.ds(0, 8 * (n_dp - 1))]
    pltpu.make_async_copy(ref, ref, recv_sems.at[4]).wait()

    same = jnp.zeros((n_dp, 128), F32)
    cross = jnp.zeros((n_dp, 128), F32)
    square = jnp.zeros((n_dp, 128), F32)
    for i in range(8):
        rows_i = slices[pl.ds(i, n_dp, stride=8), :]
        same = same + rows_i * mine[i : i + 1]
        cross = cross + rows_i * swapped[i : i + 1]
        square = square + rows_i * rows_i
    stack = jnp.concatenate([same, cross, square, jnp.zeros((n_dp, 128), F32)], axis=0)
    partial = dot_t(halves, stack, HIGH)
    sum_src[...] = partial
    sums[me_v] = partial
    send_v(lambda to: sum_src, sums, 5)
    wait_blocks(sums, recv_sems.at[5], n_voc)
    total = jnp.sum(sums[...], axis=0)

    root = lax.rsqrt(total + 1e-6)
    root_same = jnp.concatenate(
        [root[:, 64:96], root[:, 64:96], jnp.zeros((8, 64), F32)], axis=1
    )
    scaled = total * root_same
    found = jnp.dot(scaled, place, precision=HIGH, preferred_element_type=F32)
    own = lax.broadcasted_iota(jnp.int32, (8, 128), 1) == 64 + me_d
    own_root = jnp.sum(jnp.where(own, root, 0.0), axis=1, keepdims=True)
    first = jnp.where(query_odd, found[1:2, 64:], found[0:1, :64]) * own_root[0:1]
    second = jnp.where(query_odd, found[1:2, :64], found[0:1, 64:]) * own_root[1:2]
    out_ref[...] = jnp.concatenate([first, second], axis=0)

    wait_blocks(in_part, send_sems.at[0], n_voc)
    wait_blocks(in_full, send_sems.at[1], n_voc)
    wait_blocks(stats, send_sems.at[2], n_voc)
    wait_blocks(eg_src, send_sems.at[3], n_voc)
    ref = slices.at[pl.ds(0, 8 * (n_dp - 1))]
    pltpu.make_async_copy(ref, ref, send_sems.at[4]).wait()
    wait_blocks(sums, send_sems.at[5], n_voc)


def solution(mesh):
    n_dp, n_voc = mesh.shape["dp"], mesh.shape["vocab"]

    def body(hidden_states, logits, targets, input_proj, output_proj, query_ids):
        tokens, rows = logits.shape
        feats = hidden_states.shape[1]
        r_in, r_out = input_proj.shape[1], output_proj.shape[1]
        examples = tokens // SEQ
        lanes = examples * r_out
        n_chunks = -(-rows // CHUNK)
        hbm = pl.BlockSpec(memory_space=pl.ANY)
        vmem = pl.BlockSpec(memory_space=pltpu.VMEM)
        block = r_in // n_voc
        return pl.pallas_call(
            functools.partial(kernel, n_dp, n_voc),
            out_shape=jax.ShapeDtypeStruct((examples, query_ids.shape[0]), F32),
            in_specs=[hbm, hbm, hbm, hbm, vmem, vmem],
            out_specs=vmem,
            scratch_shapes=[
                pltpu.VMEM((rows, tokens), BF16),
                pltpu.VMEM((rows, tokens), F32),
                pltpu.VMEM((r_out, rows), BF16),
                pltpu.VMEM((tokens, feats), BF16),
                pltpu.VMEM((r_in, feats), BF16),
                pltpu.VMEM((n_voc, block, tokens), F32),
                pltpu.VMEM((n_voc, block, tokens), F32),
                pltpu.VMEM((block, tokens), F32),
                pltpu.VMEM((n_voc, block, tokens), F32),
                pltpu.VMEM((8, 128), F32),
                pltpu.VMEM((n_voc, 8, 128), F32),
                pltpu.VMEM((n_voc, block, lanes), F32),
                pltpu.VMEM((n_voc, block, lanes), F32),
                pltpu.VMEM((block, lanes), F32),
                pltpu.VMEM((n_dp * block, lanes), F32),
                pltpu.VMEM((8, 128), F32),
                pltpu.VMEM((n_voc, 8, 128), F32),
                pltpu.SemaphoreType.DMA((3,)),
                pltpu.SemaphoreType.DMA((n_chunks,)),
                pltpu.SemaphoreType.DMA((6,)),
                pltpu.SemaphoreType.DMA((6,)),
            ],
            compiler_params=pltpu.CompilerParams(
                collective_id=0,
                has_side_effects=True,
                vmem_limit_bytes=56 * 1024 * 1024,
            ),
            cost_estimate=pl.CostEstimate(
                flops=2 * tokens * rows * r_out,
                bytes_accessed=2 * (tokens * rows + rows * r_out),
                transcendentals=tokens * rows,
            ),
        )(
            logits.T,
            output_proj.T,
            hidden_states,
            input_proj.T,
            targets.reshape(1, tokens),
            query_ids.reshape(1, -1),
        )

    return jax.shard_map(
        body,
        mesh=mesh,
        in_specs=(
            P("dp", "vocab"),
            P("dp", "vocab"),
            P("dp"),
            P("vocab", None),
            P("vocab", None),
            P(),
        ),
        out_specs=P("dp", None),
        check_vma=False,
    )
```

```python
import functools

import jax
import jax.numpy as jnp
from jax import lax
from jax.experimental import pallas as pl
from jax.experimental.pallas import tpu as pltpu
from jax.sharding import PartitionSpec as P

MESH = pl.DeviceIdType.MESH
F32 = jnp.float32
BF16 = jnp.bfloat16
SEQ = 128
LOG2E = 1.4426950408889634
HIGH = lax.Precision.HIGHEST
CHUNK = 2048
BLOCK = 256
LANES = 32
MSG = 24


def dot(a, b, precision=None):
    return jnp.dot(a, b, precision=precision, preferred_element_type=F32)


def dot_t(a, b, precision=None):
    return lax.dot_general(
        a, b, (((1,), (1,)), ((), ())), precision=precision, preferred_element_type=F32
    )


def ring(step, size):
    return min(step, size - step)


def kernel(
    n_x,
    n_z,
    n_y,
    logits_hbm,
    proj_hbm,
    hidden_hbm,
    inproj_hbm,
    targets_ref,
    query_ref,
    out_ref,
    lbuf,
    pbuf,
    hbuf,
    ibuf,
    in_part,
    in_parts,
    in_block,
    in_full,
    msg_src,
    msgs,
    hit_src,
    hits,
    slice_src,
    slices,
    sum_src,
    sums,
    load_sems,
    logit_sems,
    proj_sems,
    send_sems,
    recv_sems,
):
    rows, tokens = lbuf.shape
    n_dp, n_voc = n_x * n_z, n_y * 2
    me_d = lax.axis_index("dp")
    me_v = lax.axis_index("vocab")
    my_x, my_z = lax.div(me_d, n_z), lax.rem(me_d, n_z)
    my_y, my_core = lax.div(me_v, 2), lax.rem(me_v, 2)
    starts = list(range(0, rows, CHUNK))
    sizes = [min(CHUNK, rows - s) for s in starts]

    load_hidden = pltpu.make_async_copy(hidden_hbm, hbuf, load_sems.at[0])
    load_inproj = pltpu.make_async_copy(inproj_hbm, ibuf, load_sems.at[1])
    load_hidden.start()
    load_inproj.start()
    chunk_loads = []
    for c, (s, w) in enumerate(zip(starts, sizes)):
        pair = (
            pltpu.make_async_copy(
                proj_hbm.at[:, pl.ds(s, w)], pbuf.at[:, pl.ds(s, w)], proj_sems.at[c]
            ),
            pltpu.make_async_copy(
                logits_hbm.at[pl.ds(s, w)], lbuf.at[pl.ds(s, w)], logit_sems.at[c]
            ),
        )
        for copy in pair:
            copy.start()
        chunk_loads.append(pair)

    steps_v = sorted(
        [(dy, dc) for dy in range(n_y) for dc in range(2) if dy or dc],
        key=lambda s: -ring(s[0], n_y),
    )
    steps_d = sorted(
        [(dx, dz) for dx in range(n_x) for dz in range(n_z) if dx or dz],
        key=lambda s: -ring(s[0], n_x) - ring(s[1], n_z),
    )
    others_v = [
        lax.rem(my_y + dy, n_y) * 2 + lax.rem(my_core + dc, 2) for dy, dc in steps_v
    ]
    others_d = [
        lax.rem(my_x + dx, n_x) * n_z + lax.rem(my_z + dz, n_z) for dx, dz in steps_d
    ]

    barrier = pltpu.get_barrier_semaphore()
    for to in others_d:
        pl.semaphore_signal(barrier, inc=1, device_id=(to, me_v), device_id_type=MESH)
    for to in others_v:
        pl.semaphore_signal(barrier, inc=1, device_id=(me_d, to), device_id_type=MESH)

    def send_v(src_of, dst, rnd):
        for to in others_v:
            pltpu.make_async_remote_copy(
                src_ref=src_of(to),
                dst_ref=dst.at[me_v],
                send_sem=send_sems.at[rnd],
                recv_sem=recv_sems.at[rnd],
                device_id=(me_d, to),
                device_id_type=MESH,
            ).start()

    def wait_blocks(dst, sem, n):
        ref = dst.at[pl.ds(0, n - 1)]
        pltpu.make_async_copy(ref, ref, sem).wait()

    load_hidden.wait()
    load_inproj.wait()
    part = dot_t(ibuf[...], hbuf[...])
    in_part[...] = part.reshape(in_part.shape)
    in_parts[me_v] = in_part[me_v]

    pl.semaphore_wait(barrier, n_voc + n_dp - 2)
    send_v(lambda to: in_part.at[to], in_parts, 0)

    tgt = targets_ref[...] - me_v * rows
    block_of = tgt >> 8
    pick = lax.broadcasted_iota(jnp.int32, (BLOCK, tokens), 0) == (tgt & 255)
    pick = pick.astype(F32).astype(BF16)

    def wait_chunk(c):
        for copy in chunk_loads[c]:
            copy.wait()

    def largest(c):
        s, w = starts[c], sizes[c]
        x = lbuf[pl.ds(s, w), :]
        tops = [x[16 * j : 16 * j + 16] for j in range(4)]
        for j in range(4, w // 16):
            tops[j % 4] = jnp.maximum(tops[j % 4], x[16 * j : 16 * j + 16])
        top = jnp.maximum(jnp.maximum(tops[0], tops[1]), jnp.maximum(tops[2], tops[3]))
        return jnp.max(top.astype(F32), axis=0, keepdims=True)

    r_out = pbuf.shape[0]
    run_sum = jnp.zeros((LANES, tokens), F32)
    out_part = jnp.zeros((r_out, tokens), F32)
    wanted = jnp.zeros((r_out, tokens), F32)
    wait_chunk(0)
    run_max = largest(0)
    for c, (s, w) in enumerate(zip(starts, sizes)):
        last = c + 1 == len(starts)
        if not last:
            wait_chunk(c + 1)
            next_max = jnp.maximum(run_max, largest(c + 1))
        terms = jnp.exp2((lbuf[pl.ds(s, w), :].astype(F32) - run_max) * LOG2E)
        parts = [terms[i : i + LANES] for i in range(0, w, LANES)]
        while len(parts) > 1:
            pairs = [a + b for a, b in zip(parts[::2], parts[1::2])]
            parts = pairs + parts[len(pairs) * 2 :]
        run_sum = run_sum + parts[0]
        out_part = out_part + dot(pbuf[:, pl.ds(s, w)], terms.astype(BF16))
        n_blocks = w // BLOCK
        cols = [pbuf[:, pl.ds(s + BLOCK * i, BLOCK)] for i in range(n_blocks)]
        found = dot(jnp.concatenate(cols, axis=0), pick)
        for i in range(n_blocks):
            here = block_of == (s // BLOCK + i)
            wanted = jnp.where(here, found[r_out * i : r_out * (i + 1)], wanted)
        rest = w % BLOCK
        if rest:
            at = s + n_blocks * BLOCK
            found = dot(pbuf[:, pl.ds(at, rest)], pick[:rest])
            wanted = jnp.where(block_of == at // BLOCK, found, wanted)
        if not last:
            shrink = jnp.exp2((run_max - next_max) * LOG2E)
            out_part = out_part * shrink
            run_sum = run_sum * shrink
            run_max = next_max
        if c == len(starts) - 3:
            wait_blocks(in_parts, recv_sems.at[0], n_voc)
            block = jnp.sum(in_parts[...], axis=0)
            in_block[...] = block
            in_full[me_v] = block
            send_v(lambda to: in_block, in_full, 1)

    total_here = jnp.sum(run_sum, axis=0, keepdims=True)
    each = r_out // n_voc
    halves = [slice(0, 128), slice(128, 256)]
    for k, half in enumerate(halves):
        msg_src[:, each * k : each * (k + 1), :] = out_part[:, half].reshape(
            n_voc, each, 128
        )
    stat_rows = [run_max[:, halves[0]], run_max[:, halves[1]]]
    stat_rows += [total_here[:, halves[0]], total_here[:, halves[1]]]
    stat_rows = jnp.concatenate(stat_rows + [jnp.zeros((4, 128), F32)], axis=0)
    msg_src[:, 2 * each : 2 * each + 8, :] = jnp.broadcast_to(
        stat_rows[None], (n_voc, 8, 128)
    )
    send_v(lambda to: msg_src.at[to], msgs, 2)
    hit_rows = jnp.concatenate(
        [wanted[:, half].reshape(n_voc, each, 128) for half in halves], axis=1
    )
    hit_src[...] = hit_rows.astype(BF16)
    send_v(lambda to: hit_src.at[to], hits, 3)
    msgs[me_v] = msg_src[me_v]
    hits[me_v] = hit_src[me_v]

    query = query_ref[...]
    query_d = query >> 1
    query_odd = (query & 1) == 1
    lane = lax.broadcasted_iota(jnp.int32, (128, 64), 0)
    place = jnp.concatenate(
        [(lane == query_d).astype(F32), (lane == query_d + n_dp).astype(F32)], axis=1
    )
    half_of = lax.broadcasted_iota(jnp.int32, (8, 128), 1) // 64
    sum_halves = (half_of == lax.broadcasted_iota(jnp.int32, (8, 128), 0)).astype(F32)

    wait_blocks(in_full, recv_sems.at[1], n_voc)
    in_low = in_full[...].reshape(in_full.shape[0] * in_full.shape[1], tokens)
    wait_blocks(msgs, recv_sems.at[2], n_voc)
    wait_blocks(hits, recv_sems.at[3], n_voc)
    mine = []
    for k, half in enumerate(halves):
        maxima = msgs[:, 2 * each + k, :]
        row_max = jnp.max(maxima, axis=0, keepdims=True)
        weight = jnp.exp2((maxima - row_max) * LOG2E)
        row_total = jnp.sum(msgs[:, 2 * each + 2 + k, :] * weight, axis=0, keepdims=True)
        weight = weight / row_total
        out_low = jnp.zeros((each, 128), F32)
        hit = jnp.zeros((each, 128), F32)
        for v in range(n_voc):
            out_low = out_low + msgs[v, each * k : each * (k + 1), :] * weight[v : v + 1]
            hit = hit + hits[v].astype(F32)[each * k : each * (k + 1)]
        mine.append(dot_t(out_low - hit, in_low[:, half], HIGH))
    mine = jnp.concatenate(mine, axis=1)
    slice_src[...] = mine
    my_rows = pl.ds(pl.multiple_of(me_d * 8, 8), 8)
    for to in others_d:
        pltpu.make_async_remote_copy(
            src_ref=slice_src,
            dst_ref=slices.at[my_rows],
            send_sem=send_sems.at[4],
            recv_sem=recv_sems.at[4],
            device_id=(to, me_v),
            device_id_type=MESH,
        ).start()
    slices[my_rows, :] = mine
    swapped = jnp.concatenate([mine[:, 64:], mine[:, :64]], axis=1)
    ref = slices.at[pl.ds(0, 8 * (n_dp - 1))]
    pltpu.make_async_copy(ref, ref, recv_sems.at[4]).wait()

    same = jnp.zeros((n_dp, 128), F32)
    cross = jnp.zeros((n_dp, 128), F32)
    square = jnp.zeros((n_dp, 128), F32)
    for i in range(8):
        rows_i = slices[pl.ds(i, n_dp, stride=8), :]
        same = same + rows_i * mine[i : i + 1]
        cross = cross + rows_i * swapped[i : i + 1]
        square = square + rows_i * rows_i
    stack = jnp.concatenate([same, cross, square, jnp.zeros((n_dp, 128), F32)], axis=0)
    partial = dot_t(sum_halves, stack, HIGH)
    sum_src[...] = partial
    send_v(lambda to: sum_src, sums, 5)
    sums[me_v] = partial
    wait_blocks(sums, recv_sems.at[5], n_voc)
    total = jnp.sum(sums[...], axis=0)

    root = lax.rsqrt(total + 1e-6)
    root_same = jnp.concatenate(
        [root[:, 64:96], root[:, 64:96], jnp.zeros((8, 64), F32)], axis=1
    )
    found = dot(total * root_same, place, HIGH)
    own = lax.broadcasted_iota(jnp.int32, (8, 128), 1) == 2 * n_dp + me_d
    own_root = jnp.sum(jnp.where(own, root, 0.0), axis=1, keepdims=True)
    first = jnp.where(query_odd, found[1:2, 64:], found[0:1, :64]) * own_root[0:1]
    second = jnp.where(query_odd, found[1:2, :64], found[0:1, 64:]) * own_root[1:2]
    out_ref[...] = jnp.concatenate([first, second], axis=0)

    wait_blocks(in_part, send_sems.at[0], n_voc)
    wait_blocks(in_full, send_sems.at[1], n_voc)
    wait_blocks(msgs, send_sems.at[2], n_voc)
    wait_blocks(hits, send_sems.at[3], n_voc)
    ref = slices.at[pl.ds(0, 8 * (n_dp - 1))]
    pltpu.make_async_copy(ref, ref, send_sems.at[4]).wait()
    wait_blocks(sums, send_sems.at[5], n_voc)


def solution(mesh):
    n_dp, n_voc = mesh.shape["dp"], mesh.shape["vocab"]
    n_x, n_z, n_y = 4, 8, 4

    def body(hidden_states, logits, targets, input_proj, output_proj, query_ids):
        tokens, rows = logits.shape
        feats = hidden_states.shape[1]
        r_in, r_out = input_proj.shape[1], output_proj.shape[1]
        examples = tokens // SEQ
        lanes = examples * r_in
        n_chunks = -(-rows // CHUNK)
        hbm = pl.BlockSpec(memory_space=pl.ANY)
        vmem = pl.BlockSpec(memory_space=pltpu.VMEM)
        in_block = r_in // n_voc
        out_block = r_out // n_voc
        return pl.pallas_call(
            functools.partial(kernel, n_x, n_z, n_y),
            out_shape=jax.ShapeDtypeStruct((examples, query_ids.shape[0]), F32),
            in_specs=[hbm, hbm, hbm, hbm, vmem, vmem],
            out_specs=vmem,
            scratch_shapes=[
                pltpu.VMEM((rows, tokens), BF16),
                pltpu.VMEM((r_out, rows), BF16),
                pltpu.VMEM((tokens, feats), BF16),
                pltpu.VMEM((r_in, feats), BF16),
                pltpu.VMEM((n_voc, in_block, tokens), F32),
                pltpu.VMEM((n_voc, in_block, tokens), F32),
                pltpu.VMEM((in_block, tokens), F32),
                pltpu.VMEM((n_voc, in_block, tokens), F32),
                pltpu.VMEM((n_voc, MSG, 128), F32),
                pltpu.VMEM((n_voc, MSG, 128), F32),
                pltpu.VMEM((n_voc, 2 * out_block, 128), BF16),
                pltpu.VMEM((n_voc, 2 * out_block, 128), BF16),
                pltpu.VMEM((out_block, lanes), F32),
                pltpu.VMEM((n_dp * out_block, lanes), F32),
                pltpu.VMEM((8, 128), F32),
                pltpu.VMEM((n_voc, 8, 128), F32),
                pltpu.SemaphoreType.DMA((2,)),
                pltpu.SemaphoreType.DMA((n_chunks,)),
                pltpu.SemaphoreType.DMA((n_chunks,)),
                pltpu.SemaphoreType.DMA((6,)),
                pltpu.SemaphoreType.DMA((6,)),
            ],
            compiler_params=pltpu.CompilerParams(
                collective_id=0,
                has_side_effects=True,
                vmem_limit_bytes=56 * 1024 * 1024,
            ),
            cost_estimate=pl.CostEstimate(
                flops=2 * tokens * rows * r_out,
                bytes_accessed=2 * (tokens * rows + rows * r_out),
                transcendentals=tokens * rows,
            ),
        )(
            logits.T,
            output_proj.T,
            hidden_states,
            input_proj.T,
            targets.reshape(1, tokens),
            query_ids.reshape(1, -1),
        )

    return jax.shard_map(
        body,
        mesh=mesh,
        in_specs=(
            P("dp", "vocab"),
            P("dp", "vocab"),
            P("dp"),
            P("vocab", None),
            P("vocab", None),
            P(),
        ),
        out_specs=P("dp", None),
        check_vma=False,
    )
```

```python
import functools

import jax
import jax.numpy as jnp
from jax import lax
from jax.experimental import pallas as pl
from jax.experimental.pallas import tpu as pltpu
from jax.sharding import PartitionSpec as P

MESH = pl.DeviceIdType.MESH
F32 = jnp.float32
BF16 = jnp.bfloat16
SEQ = 128
LOG2E = 1.4426950408889634
HIGH = lax.Precision.HIGHEST
BLOCK = 256
SIZES = (2048, 2048, 2048, 2048, 2048, 2048, 2048, 1696)
INPUTS = 1
GREET = 1
SHARE = 3
HITS = 3
MSG = 40


def dot(a, b, precision=None):
    return jnp.dot(a, b, precision=precision, preferred_element_type=F32)


def dot_t(a, b, precision=None):
    return lax.dot_general(
        a, b, (((1,), (1,)), ((), ())), precision=precision, preferred_element_type=F32
    )


def ring(step, size):
    return min(step, size - step)


def kernel(
    n_x,
    n_z,
    n_y,
    logits_hbm,
    proj_hbm,
    hidden_hbm,
    inproj_hbm,
    targets_hbm,
    query_hbm,
    out_ref,
    targets_ref,
    query_ref,
    lbuf,
    pbuf,
    hbuf,
    ibuf,
    in_part,
    in_pair,
    in_sum,
    in_sums,
    msg_src,
    msgs,
    hit_src,
    hits,
    slice_src,
    slices,
    sum_src,
    sums,
    load_sems,
    logit_sems,
    proj_sems,
    send_sems,
    recv_sems,
):
    rows, tokens = lbuf.shape
    n_dp, n_voc = n_x * n_z, n_y * 2
    me_d = lax.axis_index("dp")
    me_v = lax.axis_index("vocab")
    my_x, my_z = lax.div(me_d, n_z), lax.rem(me_d, n_z)
    my_y, my_core = lax.div(me_v, 2), lax.rem(me_v, 2)
    sizes = SIZES
    starts = [sum(sizes[:c]) for c in range(len(sizes))]
    n_chunks = len(sizes)

    load_hidden = pltpu.make_async_copy(hidden_hbm, hbuf, load_sems.at[0])
    load_inproj = pltpu.make_async_copy(inproj_hbm, ibuf, load_sems.at[1])
    r_out = proj_hbm.shape[0]
    proj_loads = [
        pltpu.make_async_copy(
            proj_hbm.at[:, pl.ds(s, w)],
            pbuf.at[pl.ds(0, r_out), pl.ds(s, w)],
            proj_sems.at[c],
        )
        for c, (s, w) in enumerate(zip(starts, sizes))
    ]
    logit_loads = [
        pltpu.make_async_copy(
            logits_hbm.at[pl.ds(s, w)], lbuf.at[pl.ds(s, w)], logit_sems.at[c]
        )
        for c, (s, w) in enumerate(zip(starts, sizes))
    ]
    load_targets = pltpu.make_async_copy(targets_hbm, targets_ref, load_sems.at[2])
    load_query = pltpu.make_async_copy(query_hbm, query_ref, load_sems.at[3])
    load_targets.start()
    for c in range(n_chunks):
        for copy in proj_loads[2 * c : 2 * c + 2]:
            copy.start()
        logit_loads[c].start()
        if c == 0:
            load_hidden.start()
            load_inproj.start()
            load_query.start()

    steps_v = sorted(
        [(dy, dc) for dy in range(n_y) for dc in range(2) if dy or dc],
        key=lambda s: -ring(s[0], n_y),
    )
    steps_d = sorted(
        [(dx, dz) for dx in range(n_x) for dz in range(n_z) if dx or dz],
        key=lambda s: -ring(s[0], n_x) - ring(s[1], n_z),
    )
    others_v = [
        lax.rem(my_y + dy, n_y) * 2 + lax.rem(my_core + dc, 2) for dy, dc in steps_v
    ]
    others_d = [
        lax.rem(my_x + dx, n_x) * n_z + lax.rem(my_z + dz, n_z) for dx, dz in steps_d
    ]

    barrier = pltpu.get_barrier_semaphore()
    for to in others_d:
        pl.semaphore_signal(barrier, inc=1, device_id=(to, me_v), device_id_type=MESH)
    for to in others_v:
        pl.semaphore_signal(barrier, inc=1, device_id=(me_d, to), device_id_type=MESH)

    def remote(src_ref, dst_ref, rnd, to):
        return pltpu.make_async_remote_copy(
            src_ref=src_ref,
            dst_ref=dst_ref,
            send_sem=send_sems.at[rnd],
            recv_sem=recv_sems.at[rnd],
            device_id=to,
            device_id_type=MESH,
        )

    def send_v(src_of, dst, rnd):
        for to in others_v:
            remote(src_of(lax.div(to, 2)), dst.at[me_v], rnd, (me_d, to)).start()

    def wait_blocks(dst, sem, n):
        ref = dst.at[pl.ds(0, n - 1)]
        pltpu.make_async_copy(ref, ref, sem).wait()

    pbuf[r_out:, :] = jnp.ones((pbuf.shape[0] - r_out, rows), BF16)

    def project_inputs():
        load_hidden.wait()
        load_inproj.wait()
        in_part[...] = dot_t(ibuf[...], hbuf[...]).reshape(in_part.shape)

    other_core = 1 - my_core
    swap_halves = remote(
        in_part.at[other_core], in_pair, 0, (me_d, my_y * 2 + other_core)
    )

    def greet():
        pl.semaphore_wait(barrier, n_voc + n_dp - 2)
        swap_halves.start()

    def share_inputs():
        swap_halves.wait_recv()
        both = in_part[my_core] + in_pair[...]
        in_sum[...] = both
        in_sums[my_y] = both
        for dy in (n_y // 2, 1, n_y - 1):
            to = lax.rem(my_y + dy, n_y) * 2 + my_core
            remote(in_sum, in_sums.at[my_y], 1, (me_d, to)).start()

    load_targets.wait()
    tgt = targets_ref[...] - me_v * rows
    block_of = tgt >> 8
    pick = lax.broadcasted_iota(jnp.int32, (BLOCK, tokens), 0) == (tgt & 255)
    pick = pick.astype(F32).astype(BF16)

    def largest(c):
        s, w = starts[c], sizes[c]
        x = lbuf[pl.ds(s, w), :]
        tops = [x[16 * j : 16 * j + 16] for j in range(4)]
        for j in range(4, w // 16):
            tops[j % 4] = jnp.maximum(tops[j % 4], x[16 * j : 16 * j + 16])
        top = jnp.maximum(jnp.maximum(tops[0], tops[1]), jnp.maximum(tops[2], tops[3]))
        return jnp.max(top.astype(F32), axis=0, keepdims=True)

    def gather(c, wanted):
        s, w = starts[c], sizes[c]
        n_blocks = w // BLOCK
        cols = [pbuf[:r_out, pl.ds(s + BLOCK * i, BLOCK)] for i in range(n_blocks)]
        found = dot(jnp.concatenate(cols, axis=0), pick)
        for i in range(n_blocks):
            here = block_of == (s // BLOCK + i)
            wanted = jnp.where(here, found[r_out * i : r_out * (i + 1)], wanted)
        rest = w % BLOCK
        if rest:
            at = s + n_blocks * BLOCK
            found = dot(pbuf[:r_out, pl.ds(at, rest)], pick[:rest])
            wanted = jnp.where(block_of == at // BLOCK, found, wanted)
        return wanted

    out_part = jnp.zeros((pbuf.shape[0], tokens), F32)
    wanted = jnp.zeros((r_out, tokens), F32)
    each = r_out // n_y
    halves = [slice(0, 128), slice(128, 256)]
    logit_loads[0].wait()
    run_max = largest(0)
    for c, (s, w) in enumerate(zip(starts, sizes)):
        last = c + 1 == n_chunks
        for copy in proj_loads[2 * c : 2 * c + 2]:
            copy.wait()
        if not last:
            logit_loads[c + 1].wait()
            next_max = jnp.maximum(run_max, largest(c + 1))
        terms = jnp.exp2((lbuf[pl.ds(s, w), :].astype(F32) - run_max) * LOG2E)
        out_part = out_part + dot(pbuf[:, pl.ds(s, w)], terms.astype(BF16))
        for piece in range(2 * c, min(2 * c + 2, n_chunks)):
            wanted = gather(piece, wanted)
        if not last:
            out_part = out_part * jnp.exp2((run_max - next_max) * LOG2E)
            run_max = next_max
        if c == INPUTS:
            project_inputs()
        if c == GREET:
            greet()
        if c == HITS:
            for k, half in enumerate(halves):
                hit_src[:, each * k : each * (k + 1), :] = (
                    wanted[:, half].reshape(n_y, each, 128).astype(BF16)
                )
            send_v(lambda to: hit_src.at[to], hits, 3)
            hits[me_v] = hit_src[my_y]
        if c == SHARE:
            share_inputs()

    for k, half in enumerate(halves):
        msg_src[:, each * k : each * (k + 1), :] = out_part[:r_out, half].reshape(
            n_y, each, 128
        )
    total_here = out_part[r_out : r_out + 1]
    stat_rows = [run_max[:, halves[0]], run_max[:, halves[1]]]
    stat_rows += [total_here[:, halves[0]], total_here[:, halves[1]]]
    stat_rows = jnp.concatenate(stat_rows + [jnp.zeros((4, 128), F32)], axis=0)
    msg_src[:, 2 * each : 2 * each + 8, :] = jnp.broadcast_to(
        stat_rows[None], (n_y, 8, 128)
    )
    send_v(lambda to: msg_src.at[to], msgs, 2)
    msgs[me_v] = msg_src[my_y]

    load_query.wait()
    query = query_ref[...]
    query_d = query >> 1
    query_odd = (query & 1) == 1
    lane = lax.broadcasted_iota(jnp.int32, (128, 64), 0)
    place = jnp.concatenate(
        [(lane == query_d).astype(F32), (lane == query_d + n_dp).astype(F32)], axis=1
    )
    half_of = (lax.broadcasted_iota(jnp.int32, (8, 128), 1) >> 5) & 1
    sum_halves = (half_of == lax.broadcasted_iota(jnp.int32, (8, 128), 0)).astype(F32)

    wait_blocks(in_sums, recv_sems.at[1], n_y)
    in_low = jnp.sum(in_sums[...], axis=0)
    wait_blocks(msgs, recv_sems.at[2], n_voc)
    wait_blocks(hits, recv_sems.at[3], n_voc)
    mine = []
    for k, half in enumerate(halves):
        maxima = msgs[:, 2 * each + k, :]
        row_max = jnp.max(maxima, axis=0, keepdims=True)
        weight = jnp.exp2((maxima - row_max) * LOG2E)
        row_total = jnp.sum(msgs[:, 2 * each + 2 + k, :] * weight, axis=0, keepdims=True)
        weight = weight / row_total
        out_low = jnp.zeros((each, 128), F32)
        hit = jnp.zeros((each, 128), F32)
        for v in range(n_voc):
            out_low = out_low + msgs[v, each * k : each * (k + 1), :] * weight[v : v + 1]
            hit = hit + hits[v].astype(F32)[each * k : each * (k + 1)]
        mine.append(dot_t(out_low - hit, in_low[:, half], HIGH))
    top, bottom = slice(0, 8), slice(8, 16)
    one, two = mine
    mine = jnp.concatenate([one[top], two[top], one[bottom], two[bottom]], axis=1)
    swapped = jnp.concatenate([two[top], one[top], two[bottom], one[bottom]], axis=1)
    slice_src[...] = mine
    my_rows = pl.ds(pl.multiple_of(me_d * 8, 8), 8)
    for to in others_d:
        remote(slice_src, slices.at[my_rows], 4, (to, me_v)).start()
    slices[my_rows, :] = mine
    ref = slices.at[pl.ds(0, 8 * (n_dp - 1))]
    pltpu.make_async_copy(ref, ref, recv_sems.at[4]).wait()

    same = jnp.zeros((n_dp, 128), F32)
    cross = jnp.zeros((n_dp, 128), F32)
    square = jnp.zeros((n_dp, 128), F32)
    for i in range(8):
        rows_i = slices[pl.ds(i, n_dp, stride=8), :]
        same = same + rows_i * mine[i : i + 1]
        cross = cross + rows_i * swapped[i : i + 1]
        square = square + rows_i * rows_i
    stack = jnp.concatenate([same, cross, square, jnp.zeros((n_dp, 128), F32)], axis=0)
    partial = dot_t(sum_halves, stack, HIGH)
    sum_src[...] = partial
    for to in others_v:
        remote(sum_src, sums.at[me_v], 5, (me_d, to)).start()
    sums[me_v] = partial
    wait_blocks(sums, recv_sems.at[5], n_voc)
    total = jnp.sum(sums[...], axis=0)

    root = lax.rsqrt(total + 1e-6)
    root_same = jnp.concatenate(
        [root[:, 64:96], root[:, 64:96], jnp.zeros((8, 64), F32)], axis=1
    )
    found = dot(total * root_same, place, HIGH)
    own = lax.broadcasted_iota(jnp.int32, (8, 128), 1) == 2 * n_dp + me_d
    own_root = jnp.sum(jnp.where(own, root, 0.0), axis=1, keepdims=True)
    first = jnp.where(query_odd, found[1:2, 64:], found[0:1, :64]) * own_root[0:1]
    second = jnp.where(query_odd, found[1:2, :64], found[0:1, 64:]) * own_root[1:2]
    out_ref[...] = jnp.concatenate([first, second], axis=0)

    swap_halves.wait_send()
    wait_blocks(in_sums, send_sems.at[1], n_y)
    wait_blocks(msgs, send_sems.at[2], n_voc)
    wait_blocks(hits, send_sems.at[3], n_voc)
    ref = slices.at[pl.ds(0, 8 * (n_dp - 1))]
    pltpu.make_async_copy(ref, ref, send_sems.at[4]).wait()
    wait_blocks(sums, send_sems.at[5], n_voc)


def solution(mesh):
    n_dp, n_voc = mesh.shape["dp"], mesh.shape["vocab"]
    n_x, n_z, n_y = 4, 8, 4

    def body(hidden_states, logits, targets, input_proj, output_proj, query_ids):
        tokens, rows = logits.shape
        feats = hidden_states.shape[1]
        r_in, r_out = input_proj.shape[1], output_proj.shape[1]
        examples = tokens // SEQ
        lanes = 128
        n_chunks = len(SIZES)
        hbm = pl.BlockSpec(memory_space=pl.ANY)
        vmem = pl.BlockSpec(memory_space=pltpu.VMEM)
        half = r_in // 2
        out_block = r_out // n_y
        return pl.pallas_call(
            functools.partial(kernel, n_x, n_z, n_y),
            out_shape=jax.ShapeDtypeStruct((examples, query_ids.shape[0]), F32),
            in_specs=[hbm] * 6,
            out_specs=vmem,
            scratch_shapes=[
                pltpu.VMEM((1, tokens), jnp.int32),
                pltpu.VMEM((1, query_ids.shape[0]), jnp.int32),
                pltpu.VMEM((rows, tokens), BF16),
                pltpu.VMEM((r_out + 16, rows), BF16),
                pltpu.VMEM((tokens, feats), BF16),
                pltpu.VMEM((r_in, feats), BF16),
                pltpu.VMEM((2, half, tokens), F32),
                pltpu.VMEM((half, tokens), F32),
                pltpu.VMEM((half, tokens), F32),
                pltpu.VMEM((n_y, half, tokens), F32),
                pltpu.VMEM((n_y, MSG, 128), F32),
                pltpu.VMEM((n_voc, MSG, 128), F32),
                pltpu.VMEM((n_y, 2 * out_block, 128), BF16),
                pltpu.VMEM((n_voc, 2 * out_block, 128), BF16),
                pltpu.VMEM((8, lanes), F32),
                pltpu.VMEM((n_dp * 8, lanes), F32),
                pltpu.VMEM((8, 128), F32),
                pltpu.VMEM((n_voc, 8, 128), F32),
                pltpu.SemaphoreType.DMA((4,)),
                pltpu.SemaphoreType.DMA((n_chunks,)),
                pltpu.SemaphoreType.DMA((n_chunks,)),
                pltpu.SemaphoreType.DMA((6,)),
                pltpu.SemaphoreType.DMA((6,)),
            ],
            compiler_params=pltpu.CompilerParams(
                collective_id=0,
                has_side_effects=True,
                vmem_limit_bytes=56 * 1024 * 1024,
            ),
            cost_estimate=pl.CostEstimate(
                flops=2 * tokens * rows * r_out,
                bytes_accessed=2 * (tokens * rows + rows * r_out),
                transcendentals=tokens * rows,
            ),
        )(
            logits.T,
            output_proj.T,
            hidden_states,
            input_proj.T,
            targets.reshape(1, tokens),
            query_ids.reshape(1, -1),
        )

    return jax.shard_map(
        body,
        mesh=mesh,
        in_specs=(
            P("dp", "vocab"),
            P("dp", "vocab"),
            P("dp"),
            P("vocab", None),
            P("vocab", None),
            P(),
        ),
        out_specs=P("dp", None),
        check_vma=False,
    )
```

```python
import functools

import jax
import jax.numpy as jnp
from jax import lax
from jax.experimental import pallas as pl
from jax.experimental.pallas import tpu as pltpu
from jax.sharding import PartitionSpec as P

MESH = pl.DeviceIdType.MESH
F32 = jnp.float32
BF16 = jnp.bfloat16
SEQ = 128
LOG2E = 1.4426950408889634
HIGH = lax.Precision.HIGHEST
BLOCK = 256
SIZES = (2048, 2048, 2048, 2048, 2048, 2048, 2048, 1696)
INPUTS = 1
GREET = 1
SHARE = 3
HITS = 3
MSG = 40


def dot(a, b, precision=None):
    return jnp.dot(a, b, precision=precision, preferred_element_type=F32)


def dot_t(a, b, precision=None):
    return lax.dot_general(
        a, b, (((1,), (1,)), ((), ())), precision=precision, preferred_element_type=F32
    )


def ring(step, size):
    return min(step, size - step)


def kernel(
    n_x,
    n_z,
    n_y,
    logits_hbm,
    proj_hbm,
    hidden_hbm,
    inproj_hbm,
    targets_hbm,
    query_hbm,
    out_ref,
    targets_ref,
    query_ref,
    lbuf,
    pbuf,
    hbuf,
    ibuf,
    in_part,
    in_pair,
    in_sum,
    in_sums,
    msg_src,
    msgs,
    hit_src,
    hits,
    slice_src,
    slices,
    sum_src,
    sums,
    load_sems,
    logit_sems,
    proj_sems,
    send_sems,
    recv_sems,
):
    rows, tokens = lbuf.shape
    n_dp, n_voc = n_x * n_z, n_y * 2
    me_d = lax.axis_index("dp")
    me_v = lax.axis_index("vocab")
    my_x, my_z = lax.div(me_d, n_z), lax.rem(me_d, n_z)
    my_y, my_core = lax.div(me_v, 2), lax.rem(me_v, 2)
    sizes = SIZES
    starts = [sum(sizes[:c]) for c in range(len(sizes))]
    n_chunks = len(sizes)

    load_hidden = pltpu.make_async_copy(hidden_hbm, hbuf, load_sems.at[0])
    load_inproj = pltpu.make_async_copy(inproj_hbm, ibuf, load_sems.at[1])
    r_out = proj_hbm.shape[0]
    proj_loads = [
        pltpu.make_async_copy(
            proj_hbm.at[:, pl.ds(s, w)],
            pbuf.at[pl.ds(0, r_out), pl.ds(s, w)],
            proj_sems.at[c],
        )
        for c, (s, w) in enumerate(zip(starts, sizes))
    ]
    logit_loads = [
        pltpu.make_async_copy(
            logits_hbm.at[pl.ds(s, w)], lbuf.at[pl.ds(s, w)], logit_sems.at[c]
        )
        for c, (s, w) in enumerate(zip(starts, sizes))
    ]
    load_targets = pltpu.make_async_copy(targets_hbm, targets_ref, load_sems.at[2])
    load_query = pltpu.make_async_copy(query_hbm, query_ref, load_sems.at[3])
    load_targets.start()
    for c in range(n_chunks):
        for copy in proj_loads[2 * c : 2 * c + 2]:
            copy.start()
        logit_loads[c].start()
        if c == 0:
            load_hidden.start()
            load_inproj.start()
            load_query.start()

    steps_v = sorted(
        [(dy, dc) for dy in range(n_y) for dc in range(2) if dy or dc],
        key=lambda s: -ring(s[0], n_y),
    )
    steps_d = sorted(
        [(dx, dz) for dx in range(n_x) for dz in range(n_z) if dx or dz],
        key=lambda s: -ring(s[0], n_x) - ring(s[1], n_z),
    )
    others_v = [
        lax.rem(my_y + dy, n_y) * 2 + lax.rem(my_core + dc, 2) for dy, dc in steps_v
    ]
    others_d = [
        lax.rem(my_x + dx, n_x) * n_z + lax.rem(my_z + dz, n_z) for dx, dz in steps_d
    ]

    barrier = pltpu.get_barrier_semaphore()
    for to in others_d:
        pl.semaphore_signal(barrier, inc=1, device_id=(to, me_v), device_id_type=MESH)
    for to in others_v:
        pl.semaphore_signal(barrier, inc=1, device_id=(me_d, to), device_id_type=MESH)

    def remote(src_ref, dst_ref, rnd, to):
        return pltpu.make_async_remote_copy(
            src_ref=src_ref,
            dst_ref=dst_ref,
            send_sem=send_sems.at[rnd],
            recv_sem=recv_sems.at[rnd],
            device_id=to,
            device_id_type=MESH,
        )

    def send_v(src_of, dst, rnd):
        for to in others_v:
            remote(src_of(lax.div(to, 2)), dst.at[me_v], rnd, (me_d, to)).start()

    def wait_blocks(dst, sem, n):
        ref = dst.at[pl.ds(0, n - 1)]
        pltpu.make_async_copy(ref, ref, sem).wait()

    pbuf[r_out:, :] = jnp.ones((pbuf.shape[0] - r_out, rows), BF16)

    def project_inputs():
        load_hidden.wait()
        load_inproj.wait()
        in_part[...] = dot_t(ibuf[...], hbuf[...]).reshape(in_part.shape)

    other_core = 1 - my_core
    swap_halves = remote(
        in_part.at[other_core], in_pair, 0, (me_d, my_y * 2 + other_core)
    )

    def greet():
        pl.semaphore_wait(barrier, n_voc + n_dp - 2)
        swap_halves.start()

    def share_inputs():
        swap_halves.wait_recv()
        both = in_part[my_core] + in_pair[...]
        in_sum[...] = both
        in_sums[my_y] = both
        for dy in (n_y // 2, 1, n_y - 1):
            to = lax.rem(my_y + dy, n_y) * 2 + my_core
            remote(in_sum, in_sums.at[my_y], 1, (me_d, to)).start()

    load_targets.wait()
    tgt = targets_ref[...] - me_v * rows
    block_of = tgt >> 8
    pick = lax.broadcasted_iota(jnp.int32, (BLOCK, tokens), 0) == (tgt & 255)
    pick = pick.astype(F32).astype(BF16)

    def largest(c):
        s, w = starts[c], sizes[c]
        x = lbuf[pl.ds(s, w), :]
        tops = [x[16 * j : 16 * j + 16] for j in range(4)]
        for j in range(4, w // 16):
            tops[j % 4] = jnp.maximum(tops[j % 4], x[16 * j : 16 * j + 16])
        top = jnp.maximum(jnp.maximum(tops[0], tops[1]), jnp.maximum(tops[2], tops[3]))
        return jnp.max(top.astype(F32), axis=0, keepdims=True)

    def gather(c, wanted):
        s, w = starts[c], sizes[c]
        n_blocks = w // BLOCK
        cols = [pbuf[:r_out, pl.ds(s + BLOCK * i, BLOCK)] for i in range(n_blocks)]
        found = dot(jnp.concatenate(cols, axis=0), pick)
        for i in range(n_blocks):
            here = block_of == (s // BLOCK + i)
            wanted = jnp.where(here, found[r_out * i : r_out * (i + 1)], wanted)
        rest = w % BLOCK
        if rest:
            at = s + n_blocks * BLOCK
            found = dot(pbuf[:r_out, pl.ds(at, rest)], pick[:rest])
            wanted = jnp.where(block_of == at // BLOCK, found, wanted)
        return wanted

    out_part = jnp.zeros((pbuf.shape[0], tokens), F32)
    wanted = jnp.zeros((r_out, tokens), F32)
    each = r_out // n_y
    halves = [slice(0, 128), slice(128, 256)]
    logit_loads[0].wait()
    run_max = largest(0)
    for c, (s, w) in enumerate(zip(starts, sizes)):
        last = c + 1 == n_chunks
        for copy in proj_loads[2 * c : 2 * c + 2]:
            copy.wait()
        if not last:
            logit_loads[c + 1].wait()
            next_max = jnp.maximum(run_max, largest(c + 1))
        terms = jnp.exp2((lbuf[pl.ds(s, w), :].astype(F32) - run_max) * LOG2E)
        out_part = out_part + dot(pbuf[:, pl.ds(s, w)], terms.astype(BF16))
        for piece in range(2 * c, min(2 * c + 2, n_chunks)):
            wanted = gather(piece, wanted)
        if not last:
            out_part = out_part * jnp.exp2((run_max - next_max) * LOG2E)
            run_max = next_max
        if c == INPUTS:
            project_inputs()
        if c == GREET:
            greet()
        if c == HITS:
            for k, half in enumerate(halves):
                hit_src[:, each * k : each * (k + 1), :] = (
                    wanted[:, half].reshape(n_y, each, 128).astype(BF16)
                )
            send_v(lambda to: hit_src.at[to], hits, 3)
            hits[me_v] = hit_src[my_y]
        if c == SHARE:
            share_inputs()

    for k, half in enumerate(halves):
        msg_src[:, each * k : each * (k + 1), :] = out_part[:r_out, half].reshape(
            n_y, each, 128
        )
    total_here = out_part[r_out : r_out + 1]
    stat_rows = [run_max[:, halves[0]], run_max[:, halves[1]]]
    stat_rows += [total_here[:, halves[0]], total_here[:, halves[1]]]
    stat_rows = jnp.concatenate(stat_rows + [jnp.zeros((4, 128), F32)], axis=0)
    msg_src[:, 2 * each : 2 * each + 8, :] = jnp.broadcast_to(
        stat_rows[None], (n_y, 8, 128)
    )
    send_v(lambda to: msg_src.at[to], msgs, 2)
    msgs[me_v] = msg_src[my_y]

    load_query.wait()
    query = query_ref[...]
    query_d = query >> 1
    query_odd = (query & 1) == 1
    lane = lax.broadcasted_iota(jnp.int32, (128, 64), 0)
    place = jnp.concatenate(
        [(lane == query_d).astype(F32), (lane == query_d + n_dp).astype(F32)], axis=1
    )
    half_of = (lax.broadcasted_iota(jnp.int32, (8, 128), 1) >> 5) & 1
    sum_halves = (half_of == lax.broadcasted_iota(jnp.int32, (8, 128), 0)).astype(F32)

    wait_blocks(in_sums, recv_sems.at[1], n_y)
    in_low = jnp.sum(in_sums[...], axis=0)
    wait_blocks(hits, recv_sems.at[3], n_voc)
    hit_sum = jnp.sum(hits[...].astype(F32), axis=0)
    wait_blocks(msgs, recv_sems.at[2], n_voc)
    mine = []
    for k, half in enumerate(halves):
        maxima = msgs[:, 2 * each + k, :]
        row_max = jnp.max(maxima, axis=0, keepdims=True)
        weight = jnp.exp2((maxima - row_max) * LOG2E)
        row_total = jnp.sum(msgs[:, 2 * each + 2 + k, :] * weight, axis=0, keepdims=True)
        weight = weight / row_total
        out_low = jnp.zeros((each, 128), F32)
        hit = hit_sum[each * k : each * (k + 1)]
        for v in range(n_voc):
            out_low = out_low + msgs[v, each * k : each * (k + 1), :] * weight[v : v + 1]
        mine.append(dot_t(out_low - hit, in_low[:, half], HIGH))
    top, bottom = slice(0, 8), slice(8, 16)
    one, two = mine
    mine = jnp.concatenate([one[top], two[top], one[bottom], two[bottom]], axis=1)
    swapped = jnp.concatenate([two[top], one[top], two[bottom], one[bottom]], axis=1)
    slice_src[...] = mine
    my_rows = pl.ds(pl.multiple_of(me_d * 8, 8), 8)
    for to in others_d:
        remote(slice_src, slices.at[my_rows], 4, (to, me_v)).start()
    slices[my_rows, :] = mine
    ref = slices.at[pl.ds(0, 8 * (n_dp - 1))]
    pltpu.make_async_copy(ref, ref, recv_sems.at[4]).wait()

    same = jnp.zeros((n_dp, 128), F32)
    cross = jnp.zeros((n_dp, 128), F32)
    square = jnp.zeros((n_dp, 128), F32)
    for i in range(8):
        rows_i = slices[pl.ds(i, n_dp, stride=8), :]
        same = same + rows_i * mine[i : i + 1]
        cross = cross + rows_i * swapped[i : i + 1]
        square = square + rows_i * rows_i
    stack = jnp.concatenate([same, cross, square, jnp.zeros((n_dp, 128), F32)], axis=0)
    partial = dot_t(sum_halves, stack, HIGH)
    sum_src[...] = partial
    for to in others_v:
        remote(sum_src.at[pl.ds(0, 2)], sums.at[me_v, pl.ds(0, 2)], 5, (me_d, to)).start()
    sums[me_v] = partial
    ref = sums.at[pl.ds(0, n_voc - 1), pl.ds(0, 2)]
    pltpu.make_async_copy(ref, ref, recv_sems.at[5]).wait()
    total = jnp.sum(sums[:, 0:2, :], axis=0)
    total = jnp.concatenate([total, jnp.zeros((6, 128), F32)], axis=0)

    root = lax.rsqrt(total + 1e-6)
    root_same = jnp.concatenate(
        [root[:, 64:96], root[:, 64:96], jnp.zeros((8, 64), F32)], axis=1
    )
    found = dot(total * root_same, place, HIGH)
    own = lax.broadcasted_iota(jnp.int32, (8, 128), 1) == 2 * n_dp + me_d
    own_root = jnp.sum(jnp.where(own, root, 0.0), axis=1, keepdims=True)
    first = jnp.where(query_odd, found[1:2, 64:], found[0:1, :64]) * own_root[0:1]
    second = jnp.where(query_odd, found[1:2, :64], found[0:1, 64:]) * own_root[1:2]
    out_ref[...] = jnp.concatenate([first, second], axis=0)

    swap_halves.wait_send()
    wait_blocks(in_sums, send_sems.at[1], n_y)
    wait_blocks(msgs, send_sems.at[2], n_voc)
    wait_blocks(hits, send_sems.at[3], n_voc)
    ref = slices.at[pl.ds(0, 8 * (n_dp - 1))]
    pltpu.make_async_copy(ref, ref, send_sems.at[4]).wait()
    ref = sums.at[pl.ds(0, n_voc - 1), pl.ds(0, 2)]
    pltpu.make_async_copy(ref, ref, send_sems.at[5]).wait()


def solution(mesh):
    n_dp, n_voc = mesh.shape["dp"], mesh.shape["vocab"]
    n_x, n_z, n_y = 4, 8, 4

    def body(hidden_states, logits, targets, input_proj, output_proj, query_ids):
        tokens, rows = logits.shape
        feats = hidden_states.shape[1]
        r_in, r_out = input_proj.shape[1], output_proj.shape[1]
        examples = tokens // SEQ
        lanes = 128
        n_chunks = len(SIZES)
        hbm = pl.BlockSpec(memory_space=pl.ANY)
        vmem = pl.BlockSpec(memory_space=pltpu.VMEM)
        half = r_in // 2
        out_block = r_out // n_y
        return pl.pallas_call(
            functools.partial(kernel, n_x, n_z, n_y),
            out_shape=jax.ShapeDtypeStruct((examples, query_ids.shape[0]), F32),
            in_specs=[hbm] * 6,
            out_specs=vmem,
            scratch_shapes=[
                pltpu.VMEM((1, tokens), jnp.int32),
                pltpu.VMEM((1, query_ids.shape[0]), jnp.int32),
                pltpu.VMEM((rows, tokens), BF16),
                pltpu.VMEM((r_out + 16, rows), BF16),
                pltpu.VMEM((tokens, feats), BF16),
                pltpu.VMEM((r_in, feats), BF16),
                pltpu.VMEM((2, half, tokens), F32),
                pltpu.VMEM((half, tokens), F32),
                pltpu.VMEM((half, tokens), F32),
                pltpu.VMEM((n_y, half, tokens), F32),
                pltpu.VMEM((n_y, MSG, 128), F32),
                pltpu.VMEM((n_voc, MSG, 128), F32),
                pltpu.VMEM((n_y, 2 * out_block, 128), BF16),
                pltpu.VMEM((n_voc, 2 * out_block, 128), BF16),
                pltpu.VMEM((8, lanes), F32),
                pltpu.VMEM((n_dp * 8, lanes), F32),
                pltpu.VMEM((8, 128), F32),
                pltpu.VMEM((n_voc, 8, 128), F32),
                pltpu.SemaphoreType.DMA((4,)),
                pltpu.SemaphoreType.DMA((n_chunks,)),
                pltpu.SemaphoreType.DMA((n_chunks,)),
                pltpu.SemaphoreType.DMA((6,)),
                pltpu.SemaphoreType.DMA((6,)),
            ],
            compiler_params=pltpu.CompilerParams(
                collective_id=0,
                has_side_effects=True,
                vmem_limit_bytes=56 * 1024 * 1024,
            ),
            cost_estimate=pl.CostEstimate(
                flops=2 * tokens * rows * r_out,
                bytes_accessed=2 * (tokens * rows + rows * r_out),
                transcendentals=tokens * rows,
            ),
        )(
            logits.T,
            output_proj.T,
            hidden_states,
            input_proj.T,
            targets.reshape(1, tokens),
            query_ids.reshape(1, -1),
        )

    return jax.shard_map(
        body,
        mesh=mesh,
        in_specs=(
            P("dp", "vocab"),
            P("dp", "vocab"),
            P("dp"),
            P("vocab", None),
            P("vocab", None),
            P(),
        ),
        out_specs=P("dp", None),
        check_vma=False,
    )
```
